32 devices in a mesh: groups: 2 (over x), tm: 16 (over z, y, core).
Axes of the slice: x: 2, y: 2, z: 4, core: 2. Of those that a mesh axis runs over, the one named last changes fastest.
Arguments:
- sharded_latents: bfloat16 [32, 6144], P('groups', 'tm'), parts along dimension 0, may hold values from -6 to 6
- sample_frame_count: int32 [16], P('groups'), parts along dimension 0, may hold values from 5 to 8, as said below
- entry_kernel: bfloat16 [27, 16, 384], replicated, may hold values from -0.3125 to 0.3125
- entry_bias: float32 [384], replicated, may hold values from -3 to 3
- norm_scale_gain: float32 [384], replicated, may hold values from 0.25 to 1.75
- residual_kernel: bfloat16 [27, 384, 384], P(None, 'tm'), may hold values from -0.0625 to 0.0625
- residual_bias: float32 [384], replicated, may hold values from -3 to 3
Outputs:
- decoded: bfloat16 [128, 6, 16, 384], P(('groups', 'tm')), parts along dimension 0
The draws below stay inside these ranges and needn't reach their ends.
There are 2 independent parts, one for each index of `groups`. The reference program is written for one: setup_inputs(seed, part) draws one part's arguments, and reference() takes and returns one part's arrays. A program takes and returns all parts, laid end to end along the dimension named above; an argument that names none is the same for every part. Nothing has to cross between parts.
Inputs may be any that keep to these rules, and one draw needn't show every extreme that they name: `sample_frame_count`: every sample has more than half of its 8 frames valid; some sample has all of them valid.
All inputs are finite; a program needn't handle non-finite values.
Results may differ from the reference program's by a relative error of at most 0.009.
Values may be sent and summed in bfloat16 or wider, within the bound.
A program may use at most 64 MiB of HBM per device.

```python
import jax
import jax.numpy as jnp
from jax import lax

LATENT_CHANNELS = 16
C = 384
PROMPT_SAMPLES = 8
BLOCK_FRAMES = 4
LATENT_ROWS = 6
LATENT_COLUMNS = 16
FRAME_BLOCKS = 2
FRAMES = 8


def draw_sample_frame_count(key, part):
    first, second = jax.random.split(jax.random.fold_in(key, 7))
    counts = jax.random.randint(first, (PROMPT_SAMPLES,), FRAMES // 2 + 1, FRAMES + 1)
    chosen = jax.random.randint(second, (), 0, PROMPT_SAMPLES)
    return jnp.where(jnp.arange(PROMPT_SAMPLES) == chosen, FRAMES, counts).astype(jnp.int32)


def steps_of(own_key, dims, pieces, least, high):
    loudness = 1.0
    for axis_at, shards_of in pieces:
        draws = jax.random.uniform(jax.random.fold_in(jax.random.fold_in(own_key, 6), axis_at), (shards_of,), jnp.float32, least / len(pieces), high / len(pieces))
        loudness = loudness * jnp.repeat(jnp.exp(draws), dims[axis_at] // shards_of).reshape((-1,) + (1,) * (len(dims) - 1 - axis_at))
    return loudness


def scatter_about(key, dims, deviation, most, shards=(), kind=jnp.bfloat16):
    values = deviation * jax.random.normal(key, dims, jnp.float32)
    if shards:
        values = values * steps_of(key, dims, shards, -0.22, 0.18)
    return jnp.clip(values, -most, most).astype(kind)


def setup_inputs(seed: int = 0, part: int = 0) -> dict:
    seeds = jax.random.split(jax.random.key(seed), 8)
    part_splits = jax.random.split(jax.random.fold_in(seeds[7], part), 8)
    sharded_latents = scatter_about(part_splits[0], (FRAME_BLOCKS * PROMPT_SAMPLES, BLOCK_FRAMES * LATENT_CHANNELS * LATENT_ROWS * LATENT_COLUMNS), 1.0, 6.0, ((1, 16),))
    sample_frame_count = draw_sample_frame_count(jax.random.fold_in(jax.random.fold_in(seeds[7], part), 71), part)
    entry_kernel = scatter_about(seeds[2], (27, LATENT_CHANNELS, C), (27 * LATENT_CHANNELS) ** -0.5, 0.3125)
    entry_bias = scatter_about(seeds[3], (C,), 0.5, 3.0, (), jnp.float32)
    norm_scale_gain = jnp.clip(1.0 + 0.15 * jax.random.normal(seeds[4], (C,), jnp.float32), 0.25, 1.75)
    residual_kernel = scatter_about(seeds[5], (27, C, C), (27 * C) ** -0.5, 0.0625, ((1, 16),))
    residual_bias = scatter_about(seeds[6], (C,), 0.5, 3.0, (), jnp.float32)
    return {"sharded_latents": sharded_latents, "sample_frame_count": sample_frame_count, "entry_kernel": entry_kernel, "entry_bias": entry_bias, "norm_scale_gain": norm_scale_gain, "residual_kernel": residual_kernel, "residual_bias": residual_bias}


def causal_conv(frames, weight):
    frames_out = frames.shape[0] - 2
    inputs = frames.shape[3]
    padded = jnp.pad(frames, ((0, 0), (1, 1), (1, 1), (0, 0)))
    total = jnp.zeros((frames_out * LATENT_ROWS * LATENT_COLUMNS, weight.shape[2]), jnp.float32)
    for time_tap in range(3):
        for row_tap in range(3):
            for col_tap in range(3):
                window = padded[time_tap:time_tap + frames_out, row_tap:row_tap + LATENT_ROWS, col_tap:col_tap + LATENT_COLUMNS, :]
                window = window.reshape(frames_out * LATENT_ROWS * LATENT_COLUMNS, inputs)
                tap = 9 * time_tap + 3 * row_tap + col_tap
                total = total + jnp.dot(window, weight[tap], preferred_element_type=jnp.float32)
    return total

def activate(stream, norm_scale_gain):
    values = stream.astype(jnp.float32)
    scale = lax.rsqrt(lax.optimization_barrier(jnp.mean(values * values, axis=-1, keepdims=True)) + 1e-06)
    return jax.nn.silu(values * scale * norm_scale_gain).astype(jnp.bfloat16)

def reference(sharded_latents, sample_frame_count, entry_kernel, entry_bias, norm_scale_gain, residual_kernel, residual_bias):
    latent_volume = sharded_latents.reshape(FRAME_BLOCKS, PROMPT_SAMPLES, BLOCK_FRAMES, LATENT_CHANNELS, LATENT_ROWS, LATENT_COLUMNS)
    latent_volume = jnp.transpose(latent_volume, (1, 0, 2, 4, 5, 3)).reshape(PROMPT_SAMPLES, FRAMES, LATENT_ROWS, LATENT_COLUMNS, LATENT_CHANNELS)

    def decode(inputs):
        sample, count = inputs
        frames = jnp.concatenate([jnp.zeros((2, LATENT_ROWS, LATENT_COLUMNS, LATENT_CHANNELS), sample.dtype), sample], axis=0)
        stream = (causal_conv(frames, entry_kernel) + entry_bias).astype(jnp.bfloat16)
        active = activate(stream, norm_scale_gain).reshape(FRAMES, LATENT_ROWS, LATENT_COLUMNS, C)
        extended = jnp.concatenate([jnp.zeros((2, LATENT_ROWS, LATENT_COLUMNS, C), active.dtype), active], axis=0)
        branch = causal_conv(extended, residual_kernel) + residual_bias
        total = (stream.astype(jnp.float32) + branch).reshape(FRAMES, LATENT_ROWS, LATENT_COLUMNS, C)
        valid = (jnp.arange(FRAMES) < count)[:, None, None, None]
        return jnp.where(valid, total, jnp.zeros_like(total)).astype(jnp.bfloat16)
    result = lax.map(decode, (latent_volume, sample_frame_count))
    result = result.reshape(PROMPT_SAMPLES, FRAME_BLOCKS, BLOCK_FRAMES, LATENT_ROWS, LATENT_COLUMNS, C)
    result = jnp.transpose(result, (1, 0, 2, 3, 4, 5))
    return result.reshape(PROMPT_SAMPLES * FRAMES, LATENT_ROWS, LATENT_COLUMNS, C)
```

```python
import jax
import jax.numpy as jnp
import numpy as np
from jax import lax
from jax.experimental import pallas as pl
from jax.experimental.pallas import tpu as pltpu
from jax.sharding import PartitionSpec as P

LATENT_CHANNELS = 16
C = 384
PROMPT_SAMPLES = 8
BLOCK_FRAMES = 4
LATENT_ROWS = 6
LATENT_COLUMNS = 16


def from_behind(block, axis, distance):
    devices = range(lax.axis_size(axis))
    route = [(i - distance, i) for i in devices if i - distance in devices]
    return lax.ppermute(block, axis, route)


def causal_conv(frames, weight):
    frames_out = frames.shape[0] - 2
    inputs = frames.shape[3]
    padded = jnp.pad(frames, ((0, 0), (1, 1), (1, 1), (0, 0)))
    total = jnp.zeros((frames_out * LATENT_ROWS * LATENT_COLUMNS, weight.shape[2]), jnp.float32)
    for time_tap in range(3):
        for row_tap in range(3):
            for col_tap in range(3):
                window = padded[
                    time_tap : time_tap + frames_out,
                    row_tap : row_tap + LATENT_ROWS,
                    col_tap : col_tap + LATENT_COLUMNS,
                    :,
                ]
                window = window.reshape(frames_out * LATENT_ROWS * LATENT_COLUMNS, inputs)
                tap = 9 * time_tap + 3 * row_tap + col_tap
                total = total + jnp.dot(window, weight[tap], preferred_element_type=jnp.float32)
    return total


def activate(stream, norm_scale_gain):
    values = stream.astype(jnp.float32)
    scale = lax.rsqrt(jnp.mean(values * values, axis=-1, keepdims=True) + 1e-06)
    return jax.nn.silu(values * scale * norm_scale_gain).astype(jnp.bfloat16)


def to_cells(planes):
    return jnp.transpose(
        planes.reshape(planes.shape[0], LATENT_CHANNELS, LATENT_ROWS, LATENT_COLUMNS), (0, 2, 3, 1)
    )


def shards(
    sharded_latents,
    sample_frame_count,
    entry_kernel,
    entry_bias,
    norm_scale_gain,
    residual_kernel,
    residual_bias,
):
    gathered_latents = lax.all_to_all(
        sharded_latents, "tm", split_axis=0, concat_axis=1, tiled=True
    )
    latent_volume = gathered_latents.reshape(
        BLOCK_FRAMES, LATENT_CHANNELS, LATENT_ROWS * LATENT_COLUMNS
    )
    position = lax.axis_index("tm")
    block = position // PROMPT_SAMPLES
    sample = position % PROMPT_SAMPLES
    keep = block > 0
    earlier = from_behind(latent_volume, "tm", PROMPT_SAMPLES)
    earlier = jnp.where(keep, earlier, jnp.zeros_like(earlier))
    frames = to_cells(jnp.concatenate([earlier, latent_volume], axis=0))
    widened = (causal_conv(frames, entry_kernel) + entry_bias).astype(jnp.bfloat16)
    active_all = activate(widened, norm_scale_gain).reshape(
        BLOCK_FRAMES + 2, LATENT_ROWS, LATENT_COLUMNS, C
    )
    behind = jnp.where(keep, active_all[:2], jnp.zeros_like(active_all[:2]))
    extended = jnp.concatenate([behind, active_all[2:]], axis=0)
    stream = widened[2 * LATENT_ROWS * LATENT_COLUMNS :]
    kernel_all = lax.all_gather(residual_kernel, "tm", axis=1, tiled=True)
    branch = causal_conv(extended, kernel_all)
    total = (stream.astype(jnp.float32) + (branch + residual_bias)).reshape(
        BLOCK_FRAMES, LATENT_ROWS, LATENT_COLUMNS, C
    )
    limit = jnp.sum(jnp.where(jnp.arange(PROMPT_SAMPLES) == sample, sample_frame_count, 0))
    frame_index = block * BLOCK_FRAMES + jnp.arange(BLOCK_FRAMES)
    valid = (frame_index < limit)[:, None, None, None]
    return jnp.where(valid, total, jnp.zeros_like(total)).astype(jnp.bfloat16)


MESH = pl.DeviceIdType.MESH
F32, BF16 = jnp.float32, jnp.bfloat16
CELLS = LATENT_ROWS * LATENT_COLUMNS
PLANE = 128
SLICES = 3
TAPS = 7


def section_kernel(
    latq, perm, mask, entry, entry_bias, gain, residual_bias, pieces,
    out,
    lat, at, act, kept, weights, acc, done,
    lat_send, lat_recv, z_send, z_recv, p_send, p_recv, c_send, c_recv, o_send, o_recv, own,
):
    x = lax.axis_index("groups")
    me = lax.axis_index("tm")
    z, y, c = me // 4, (me // 2) % 2, me % 2
    quarter = 2 * x + c
    across = 2 * (1 - x) + c

    def where_(zz, yy, cc):
        return {"tm": zz * 4 + yy * 2 + cc}

    peers = [
        {"groups": x, "tm": z * 4 + (1 - y) * 2 + c},
        {"groups": 1 - x, "tm": me},
        {"groups": 1 - x, "tm": z * 4 + (1 - y) * 2 + c},
    ]
    sibling = {"tm": z * 4 + y * 2 + (1 - c)}

    barrier = pltpu.get_barrier_semaphore()
    for step in range(1, 16):
        pl.semaphore_signal(barrier, inc=1, device_id={"tm": lax.rem(me + step, 16)}, device_id_type=MESH)
    for peer in peers[1:]:
        pl.semaphore_signal(barrier, inc=1, device_id=peer, device_id_type=MESH)
    pl.semaphore_wait(barrier, 17)

    def remote(src, dst, send, recv, device):
        return pltpu.make_async_remote_copy(
            src_ref=src, dst_ref=dst, send_sem=send, recv_sem=recv, device_id=device, device_id_type=MESH
        )

    def lat_copy(to):
        return remote(latq.at[to % 4], lat.at[me], lat_send.at[to], lat_recv.at[me], {"tm": to})

    def rows_of(zz, yy):
        return pl.ds(pl.multiple_of(48 * (2 * zz + yy), 16), 48)

    def z_copy(n):
        return remote(
            pieces.at[n], weights.at[quarter, :, rows_of(z, y), :], z_send.at[n], z_recv.at[z], where_(n, y, c)
        )

    def z_arrival(zz):
        return remote(
            pieces.at[0], weights.at[quarter, :, rows_of(zz, y), :], z_send.at[0], z_recv.at[zz], where_(zz, y, c)
        )

    def p_copy(r, zz):
        block = weights.at[quarter, :, rows_of(zz, y), :]
        return remote(block, block, p_send.at[r, zz], p_recv.at[r, zz], peers[r])

    def p_arrival(r, zz):
        block = weights.at[quarter if r == 0 else across, :, rows_of(zz, y if r == 1 else 1 - y), :]
        return remote(block, block, p_send.at[r, zz], p_recv.at[r, zz], peers[r])

    def c_copy(i):
        block = weights.at[quarter if i == 0 else across]
        return remote(block, block, c_send.at[i], c_recv.at[i], sibling)

    def c_arrival(i):
        block = weights.at[2 * x + 1 - c if i == 0 else 2 * (1 - x) + 1 - c]
        return remote(block, block, c_send.at[i], c_recv.at[i], sibling)

    def columns(n):
        return pl.ds(pl.multiple_of(128 * n, 128), 128)

    def o_copy(d):
        return remote(done.at[d], out.at[:, columns(z)], o_send.at[d], o_recv.at[z], where_(d, y, c))

    def o_arrival(n):
        return remote(done.at[0], out.at[:, columns(n)], o_send.at[0], o_recv.at[n], where_(n, y, c))

    for to in range(12):
        @pl.when(to != me)
        def _():
            lat_copy(to).start()

    for n in range(SLICES):
        @pl.when(n != z)
        def _():
            z_copy(n).start()

    @pl.when(z < SLICES)
    def _():
        mine = [
            pltpu.make_async_copy(latq.at[me % 4], lat.at[me], own.at[0]),
            pltpu.make_async_copy(pieces.at[lax.rem(z, SLICES)], weights.at[quarter, :, rows_of(z, y), :], own.at[1]),
        ]
        for copy in mine:
            copy.start()
        at[:, 0:2] = jnp.zeros((2, 2, 144, PLANE), BF16)
        act[:, :, 0:2] = jnp.zeros((3, 2, 2, PLANE, C), BF16)
        act[:, :, 2:, 0:16] = jnp.zeros((3, 2, 8, 16, C), BF16)
        act[:, :, 2:, 112:128] = jnp.zeros((3, 2, 8, 16, C), BF16)
        mine[0].wait()
        for source in range(16):
            @pl.when(source != me)
            def _():
                remote(latq.at[0], lat.at[source], lat_send.at[0], lat_recv.at[source], {"tm": source}).wait_recv()
        cells = jnp.dot(perm[...], lat[...].reshape(256, PLANE), preferred_element_type=F32)
        lane = lax.broadcasted_iota(jnp.int32, (256, PLANE), 1)
        row, column = lane // LATENT_COLUMNS, lane % LATENT_COLUMNS
        for j in range(3):
            for k in range(3):
                offset = (j - 1) * LATENT_COLUMNS + (k - 1)
                moved = pltpu.roll(cells, (-offset) % PLANE, 1) if offset else cells
                good = (
                    (row + (j - 1) >= 0)
                    & (row + (j - 1) < LATENT_ROWS)
                    & (column + (k - 1) >= 0)
                    & (column + (k - 1) < LATENT_COLUMNS)
                )
                tap = 3 * j + k
                at[:, 2:, tap * 16 : tap * 16 + 16, :] = (
                    jnp.where(good, moved, 0.0).astype(BF16).reshape(2, 8, 16, PLANE)
                )

        def inlet(index, carry):
            h, f = index // 8, index % 8
            left = at[h, pl.ds(f, 3)].reshape(432, PLANE)
            wide = lax.dot_general(left, entry[...], (((0,), (0,)), ((), ())), preferred_element_type=F32)
            stream = (wide[:CELLS] + entry_bias[...]).astype(BF16)
            kept[index] = stream
            values = stream.astype(F32)
            scale = lax.rsqrt(jnp.mean(values * values, axis=-1, keepdims=True) + 1e-06)
            u = values * scale * gain[...]
            active = (u / (1.0 + jnp.exp(-u))).astype(BF16).astype(F32)
            column = lax.broadcasted_iota(jnp.int32, (CELLS, C), 0) % LATENT_COLUMNS
            act[1, h, 2 + f, 16:112] = active.astype(BF16)
            act[0, h, 2 + f, 16:112] = jnp.where(column == 0, 0.0, pltpu.roll(active, 1, 0)).astype(BF16)
            act[2, h, 2 + f, 16:112] = jnp.where(
                column == LATENT_COLUMNS - 1, 0.0, pltpu.roll(active, CELLS - 1, 0)
            ).astype(BF16)
            return carry

        lax.fori_loop(0, 8, inlet, 0)
        mine[1].wait()
        for zz in range(4):
            @pl.when(zz != z)
            def _():
                z_arrival(zz).wait_recv()
            for r in range(3):
                p_copy(r, zz).start()
        lax.fori_loop(8, 16, inlet, 0)

        def taps_of(which, d):
            h, b = d % 2, d // 2

            def step(t, total):
                tap = jnp.minimum(which * TAPS + t, 26)
                i, j, k = tap // 9, (tap // 3) % 3, tap % 3
                left = act[k, h, pl.ds(4 * b + i, 4), pl.ds(pl.multiple_of(16 * j, 16), CELLS), :]
                return total + jnp.dot(
                    left.reshape(4 * CELLS, C), weights[which, t], preferred_element_type=F32
                )

            return step

        def sweep(which, first):
            def body(d, carry):
                start = jnp.zeros((4 * CELLS, 128), F32) if first else acc[d]
                acc[d] = lax.fori_loop(0, TAPS, taps_of(which, d), start, unroll=True)
                return carry

            lax.fori_loop(0, 4, body, 0)

        for zz in range(4):
            p_arrival(0, zz).wait_recv()
        c_copy(0).start()
        sweep(quarter, True)
        for r in (1, 2):
            for zz in range(4):
                p_arrival(r, zz).wait_recv()
        c_copy(1).start()
        c_arrival(0).wait_recv()
        sweep(2 * x + 1 - c, False)
        sweep(across, False)
        c_arrival(1).wait_recv()
        last = 2 * (1 - x) + 1 - c

        def finish(d, carry):
            h, b = d % 2, d // 2
            total = lax.fori_loop(0, TAPS, taps_of(last, d), acc[d], unroll=True)
            stream = kept[pl.ds(h * 8 + b * 4, 4), :, columns(z)].astype(F32)
            total = stream + (total + residual_bias[0:1, columns(z)]).reshape(4, CELLS, 128)
            valid = mask[pl.ds(h * 8 + b * 4, 4)] > 0.0
            done[d] = jnp.where(valid, total, 0.0).astype(BF16).reshape(4 * CELLS, 128)

            @pl.when(d != z)
            def _():
                o_copy(d).start()

            return carry

        lax.fori_loop(0, 4, finish, 0)
        out[:, columns(z)] = done[z]

    for n in range(SLICES):
        @pl.when(n != z)
        def _():
            o_arrival(n).wait_recv()
            z_copy(n).wait_send()

    for to in range(12):
        @pl.when(to != me)
        def _():
            lat_copy(to).wait_send()

    @pl.when(z < SLICES)
    def _():
        for r in range(3):
            for zz in range(4):
                p_copy(r, zz).wait_send()
        for i in range(2):
            c_copy(i).wait_send()
        for d in range(4):
            @pl.when(d != z)
            def _():
                o_copy(d).wait_send()


def permutation():
    matrix = np.zeros((256, 256), np.float32)
    for h in range(2):
        for b in range(2):
            for g in range(4):
                for ch in range(16):
                    source = (g * 4 + ch // 4) * 16 + (b * 2 + h) * 4 + ch % 4
                    matrix[(h * 8 + b * 4 + g) * 16 + ch, source] = 1.0
    return matrix


def sliced_shards(
    sharded_latents,
    sample_frame_count,
    entry_kernel,
    entry_bias,
    norm_scale_gain,
    residual_kernel,
    residual_bias,
):
    x, me = lax.axis_index("groups"), lax.axis_index("tm")
    c = me % 2
    quarters = jnp.pad(residual_kernel, ((0, 1), (0, 0), (0, 0)))
    mine = lax.dynamic_slice_in_dim(quarters, (2 * x + c) * TAPS, TAPS, 0)
    theirs = lax.dynamic_slice_in_dim(quarters, (2 * x + 1 - c) * TAPS, TAPS, 0)
    received = lax.ppermute(theirs, "tm", [(i, i ^ 1) for i in range(16)])
    low = jnp.where(c == 0, mine, received)
    high = jnp.where(c == 0, received, mine)
    both = jnp.concatenate([low, high], axis=1)
    pieces = jnp.transpose(both.reshape(TAPS, 48, SLICES, 128), (2, 0, 1, 3))

    latq = jnp.transpose(sharded_latents.reshape(4, 4, 4, CELLS), (1, 0, 2, 3)).reshape(4, 16, CELLS)
    latq = jnp.pad(latq, ((0, 0), (0, 0), (0, PLANE - CELLS)))
    q = me % 4
    counts = jnp.stack([
        lax.dynamic_index_in_dim(sample_frame_count, q, keepdims=False),
        lax.dynamic_index_in_dim(sample_frame_count, q + 4, keepdims=False),
    ])
    mask = (jnp.arange(8)[None, :] < counts[:, None]).astype(F32).reshape(16, 1, 1)
    mask = jnp.broadcast_to(mask, (16, 1, 128))

    vmem = pl.BlockSpec(memory_space=pltpu.VMEM)
    dma = pltpu.SemaphoreType.DMA
    out = pl.pallas_call(
        section_kernel,
        out_shape=jax.ShapeDtypeStruct((4 * CELLS, C), BF16),
        in_specs=[vmem] * 8,
        out_specs=vmem,
        scratch_shapes=[
            pltpu.VMEM((16, 16, PLANE), BF16),
            pltpu.VMEM((2, 10, 144, PLANE), BF16),
            pltpu.VMEM((3, 2, 10, PLANE, C), BF16),
            pltpu.VMEM((16, CELLS, C), BF16),
            pltpu.VMEM((4, TAPS, C, 128), BF16),
            pltpu.VMEM((4, 4 * CELLS, 128), F32),
            pltpu.VMEM((4, 4 * CELLS, 128), BF16),
            dma((12,)), dma((16,)), dma((3,)), dma((4,)), dma((3, 4)), dma((3, 4)),
            dma((2,)), dma((2,)), dma((4,)), dma((3,)), dma((2,)),
        ],
        compiler_params=pltpu.CompilerParams(
            collective_id=0, has_side_effects=True, vmem_limit_bytes=40 * 1024 * 1024
        ),
        cost_estimate=pl.CostEstimate(flops=5_000_000_000, bytes_accessed=2_000_000, transcendentals=600_000),
    )(
        latq,
        jnp.asarray(permutation(), BF16),
        mask,
        entry_kernel.reshape(27 * LATENT_CHANNELS, C),
        entry_bias.reshape(1, C),
        norm_scale_gain.reshape(1, C),
        residual_bias.reshape(1, C),
        pieces,
    )
    return out.reshape(4, LATENT_ROWS, LATENT_COLUMNS, C)


def solution(mesh):
    in_specs = (P("groups", "tm"), P("groups"), P(), P(), P(), P(None, "tm", None), P())
    out_specs = P(("groups", "tm"), None, None, None)
    sliced = mesh.shape["groups"] == 2 and mesh.shape["tm"] == 16
    body = sliced_shards if sliced else shards
    return jax.shard_map(body, mesh=mesh, in_specs=in_specs, out_specs=out_specs, check_vma=False)
```

```python
import jax
import jax.numpy as jnp
from jax import lax
from jax.experimental import pallas as pl
from jax.experimental.pallas import tpu as pltpu
from jax.sharding import PartitionSpec as P

LATENT_CHANNELS = 16
C = 384
PROMPT_SAMPLES = 8
BLOCK_FRAMES = 4
LATENT_ROWS = 6
LATENT_COLUMNS = 16


def from_behind(block, axis, distance):
    devices = range(lax.axis_size(axis))
    route = [(i - distance, i) for i in devices if i - distance in devices]
    return lax.ppermute(block, axis, route)


def causal_conv(frames, weight):
    frames_out = frames.shape[0] - 2
    inputs = frames.shape[3]
    padded = jnp.pad(frames, ((0, 0), (1, 1), (1, 1), (0, 0)))
    total = jnp.zeros((frames_out * LATENT_ROWS * LATENT_COLUMNS, weight.shape[2]), jnp.float32)
    for time_tap in range(3):
        for row_tap in range(3):
            for col_tap in range(3):
                window = padded[
                    time_tap : time_tap + frames_out,
                    row_tap : row_tap + LATENT_ROWS,
                    col_tap : col_tap + LATENT_COLUMNS,
                    :,
                ]
                window = window.reshape(frames_out * LATENT_ROWS * LATENT_COLUMNS, inputs)
                tap = 9 * time_tap + 3 * row_tap + col_tap
                total = total + jnp.dot(window, weight[tap], preferred_element_type=jnp.float32)
    return total


def activate(stream, norm_scale_gain):
    values = stream.astype(jnp.float32)
    scale = lax.rsqrt(jnp.mean(values * values, axis=-1, keepdims=True) + 1e-06)
    return jax.nn.silu(values * scale * norm_scale_gain).astype(jnp.bfloat16)


def to_cells(planes):
    return jnp.transpose(
        planes.reshape(planes.shape[0], LATENT_CHANNELS, LATENT_ROWS, LATENT_COLUMNS), (0, 2, 3, 1)
    )


def shards(
    sharded_latents,
    sample_frame_count,
    entry_kernel,
    entry_bias,
    norm_scale_gain,
    residual_kernel,
    residual_bias,
):
    gathered_latents = lax.all_to_all(
        sharded_latents, "tm", split_axis=0, concat_axis=1, tiled=True
    )
    latent_volume = gathered_latents.reshape(
        BLOCK_FRAMES, LATENT_CHANNELS, LATENT_ROWS * LATENT_COLUMNS
    )
    position = lax.axis_index("tm")
    block = position // PROMPT_SAMPLES
    sample = position % PROMPT_SAMPLES
    keep = block > 0
    earlier = from_behind(latent_volume, "tm", PROMPT_SAMPLES)
    earlier = jnp.where(keep, earlier, jnp.zeros_like(earlier))
    frames = to_cells(jnp.concatenate([earlier, latent_volume], axis=0))
    widened = (causal_conv(frames, entry_kernel) + entry_bias).astype(jnp.bfloat16)
    active_all = activate(widened, norm_scale_gain).reshape(
        BLOCK_FRAMES + 2, LATENT_ROWS, LATENT_COLUMNS, C
    )
    behind = jnp.where(keep, active_all[:2], jnp.zeros_like(active_all[:2]))
    extended = jnp.concatenate([behind, active_all[2:]], axis=0)
    stream = widened[2 * LATENT_ROWS * LATENT_COLUMNS :]
    kernel_all = lax.all_gather(residual_kernel, "tm", axis=1, tiled=True)
    branch = causal_conv(extended, kernel_all)
    total = (stream.astype(jnp.float32) + (branch + residual_bias)).reshape(
        BLOCK_FRAMES, LATENT_ROWS, LATENT_COLUMNS, C
    )
    limit = jnp.sum(jnp.where(jnp.arange(PROMPT_SAMPLES) == sample, sample_frame_count, 0))
    frame_index = block * BLOCK_FRAMES + jnp.arange(BLOCK_FRAMES)
    valid = (frame_index < limit)[:, None, None, None]
    return jnp.where(valid, total, jnp.zeros_like(total)).astype(jnp.bfloat16)


MESH = pl.DeviceIdType.MESH
F32, BF16 = jnp.float32, jnp.bfloat16
CELLS = LATENT_ROWS * LATENT_COLUMNS
PLANE = 128
SLICES = 3
TAPS = 7


def section_kernel(
    latq, counts, entry_far, entry_bias_far, gain_far, residual_bias_far, pieces,
    out,
    entry, entry_bias, gain, residual_bias, lat, at, act, kept, weights, acc, done,
    lat_send, lat_recv, z_send, z_recv, p_send, p_recv, c_send, c_recv, o_send, o_recv, own,
):
    x = lax.axis_index("groups")
    me = lax.axis_index("tm")
    z, y, c = me // 4, (me // 2) % 2, me % 2
    quarter = 2 * x + c
    across = 2 * (1 - x) + c

    def where_(zz, yy, cc):
        return {"tm": zz * 4 + yy * 2 + cc}

    peers = [
        {"groups": x, "tm": z * 4 + (1 - y) * 2 + c},
        {"groups": 1 - x, "tm": me},
        {"groups": 1 - x, "tm": z * 4 + (1 - y) * 2 + c},
    ]
    sibling = {"tm": z * 4 + y * 2 + (1 - c)}

    barrier = pltpu.get_barrier_semaphore()
    for step in range(1, 16):
        pl.semaphore_signal(barrier, inc=1, device_id={"tm": lax.rem(me + step, 16)}, device_id_type=MESH)
    for peer in peers[1:]:
        pl.semaphore_signal(barrier, inc=1, device_id=peer, device_id_type=MESH)
    pl.semaphore_wait(barrier, 17)

    def remote(src, dst, send, recv, device):
        return pltpu.make_async_remote_copy(
            src_ref=src, dst_ref=dst, send_sem=send, recv_sem=recv, device_id=device, device_id_type=MESH
        )

    def lat_copy(to):
        return remote(latq.at[to % 4], lat.at[me], lat_send.at[to], lat_recv.at[me], {"tm": to})

    def rows_of(zz, yy):
        return pl.ds(pl.multiple_of(48 * (2 * zz + yy), 16), 48)

    def z_copy(n):
        return remote(
            pieces.at[n], weights.at[quarter, :, rows_of(z, y), :], z_send.at[n], z_recv.at[z], where_(n, y, c)
        )

    def z_arrival(zz):
        return remote(
            pieces.at[0], weights.at[quarter, :, rows_of(zz, y), :], z_send.at[0], z_recv.at[zz], where_(zz, y, c)
        )

    def p_copy(r, zz, source=None):
        block = weights.at[quarter, :, rows_of(zz, y), :]
        return remote(block if source is None else source, block, p_send.at[r, zz], p_recv.at[r, zz], peers[r])

    def p_arrival(r, zz):
        block = weights.at[quarter if r == 0 else across, :, rows_of(zz, y if r == 1 else 1 - y), :]
        return remote(block, block, p_send.at[r, zz], p_recv.at[r, zz], peers[r])

    def c_block(core, r, zz):
        which = 2 * (x if r < 2 else 1 - x) + core
        return weights.at[which, :, rows_of(zz, y if r % 2 == 0 else 1 - y), :]

    def c_copy(r, zz, source=None):
        block = c_block(c, r, zz)
        return remote(block if source is None else source, block, c_send.at[r, zz], c_recv.at[r, zz], sibling)

    def c_arrival(r, zz):
        block = c_block(1 - c, r, zz)
        return remote(block, block, c_send.at[r, zz], c_recv.at[r, zz], sibling)

    def columns(n):
        return pl.ds(pl.multiple_of(128 * n, 128), 128)

    def o_copy(d):
        return remote(done.at[d], out.at[:, columns(z)], o_send.at[d], o_recv.at[z], where_(d, y, c))

    def o_arrival(n):
        return remote(done.at[0], out.at[:, columns(n)], o_send.at[0], o_recv.at[n], where_(n, y, c))

    for to in range(12):
        @pl.when(to != me)
        def _():
            lat_copy(to).start()

    for n in range(SLICES):
        @pl.when(n != z)
        def _():
            z_copy(n).start()

    @pl.when(z < SLICES)
    def _():
        own_piece = pieces.at[lax.rem(z, SLICES)]
        for r in range(3):
            p_copy(r, z, own_piece).start()
        c_copy(0, z, own_piece).start()
        mine = [
            pltpu.make_async_copy(latq.at[me % 4], lat.at[me], own.at[0]),
            pltpu.make_async_copy(own_piece, weights.at[quarter, :, rows_of(z, y), :], own.at[1]),
            pltpu.make_async_copy(entry_far, entry, own.at[2]),
            pltpu.make_async_copy(entry_bias_far, entry_bias, own.at[3]),
            pltpu.make_async_copy(gain_far, gain, own.at[4]),
            pltpu.make_async_copy(residual_bias_far, residual_bias, own.at[5]),
        ]
        for copy in mine:
            copy.start()

        def forward(step):
            near = jnp.where(z == 2, 3 - step, step + jnp.where(step >= z, 1, 0))
            near = jnp.where((z == 2) & (step == 0), 3, near)
            near = jnp.where((z == 2) & (step > 0), 2 - step, near)
            z_arrival(near).wait_recv()
            for r in range(3):
                p_copy(r, near).start()
            c_copy(0, near).start()

        at[:, 0:2] = jnp.zeros((2, 2, 144, PLANE), BF16)
        act[:, :, 0:2] = jnp.zeros((3, 2, 2, PLANE, C), BF16)
        act[:, :, 2:, 0:16] = jnp.zeros((3, 2, 8, 16, C), BF16)
        act[:, :, 2:, 112:128] = jnp.zeros((3, 2, 8, 16, C), BF16)
        forward(0)
        for copy in mine:
            copy.wait()
        for source in range(16):
            @pl.when(source != me)
            def _():
                remote(latq.at[0], lat.at[source], lat_send.at[0], lat_recv.at[source], {"tm": source}).wait_recv()
        target = lax.broadcasted_iota(jnp.int32, (256, 256), 0)
        origin = lax.broadcasted_iota(jnp.int32, (256, 256), 1)
        h_, b_, g_, ch_ = target // 128, (target // 64) % 2, (target // 16) % 4, target % 16
        perm = (origin == (g_ * 4 + ch_ // 4) * 16 + (b_ * 2 + h_) * 4 + ch_ % 4).astype(F32).astype(BF16)
        cells = jnp.dot(perm, lat[...].reshape(256, PLANE), preferred_element_type=F32)
        lane = lax.broadcasted_iota(jnp.int32, (256, PLANE), 1)
        row, column = lane // LATENT_COLUMNS, lane % LATENT_COLUMNS
        for j in range(3):
            for k in range(3):
                offset = (j - 1) * LATENT_COLUMNS + (k - 1)
                moved = pltpu.roll(cells, (-offset) % PLANE, 1) if offset else cells
                good = (
                    (row + (j - 1) >= 0)
                    & (row + (j - 1) < LATENT_ROWS)
                    & (column + (k - 1) >= 0)
                    & (column + (k - 1) < LATENT_COLUMNS)
                )
                tap = 3 * j + k
                at[:, 2:, tap * 16 : tap * 16 + 16, :] = (
                    jnp.where(good, moved, 0.0).astype(BF16).reshape(2, 8, 16, PLANE)
                )

        def inlet(index, carry):
            h, f = index // 8, index % 8
            left = at[h, pl.ds(f, 3)].reshape(432, PLANE)
            wide = lax.dot_general(left, entry[...], (((0,), (0,)), ((), ())), preferred_element_type=F32)
            stream = (wide[:CELLS] + entry_bias[...][None, :]).astype(BF16)
            kept[index] = stream
            values = stream.astype(F32)
            scale = lax.rsqrt(jnp.mean(values * values, axis=-1, keepdims=True) + 1e-06)
            u = values * scale * gain[...][None, :]
            active = (u / (1.0 + jnp.exp(-u))).astype(BF16).astype(F32)
            column = lax.broadcasted_iota(jnp.int32, (CELLS, C), 0) % LATENT_COLUMNS
            act[1, h, 2 + f, 16:112] = active.astype(BF16)
            act[0, h, 2 + f, 16:112] = jnp.where(column == 0, 0.0, pltpu.roll(active, 1, 0)).astype(BF16)
            act[2, h, 2 + f, 16:112] = jnp.where(
                column == LATENT_COLUMNS - 1, 0.0, pltpu.roll(active, CELLS - 1, 0)
            ).astype(BF16)
            return carry

        lax.fori_loop(0, 4, inlet, 0)
        forward(1)
        lax.fori_loop(4, 10, inlet, 0)
        forward(2)
        lax.fori_loop(10, 16, inlet, 0)

        def taps_of(which, d):
            h, b = d % 2, d // 2

            def step(t, total):
                tap = jnp.minimum(which * TAPS + t, 26)
                i, j, k = tap // 9, (tap // 3) % 3, tap % 3
                left = act[k, h, pl.ds(4 * b + i, 4), pl.ds(pl.multiple_of(16 * j, 16), CELLS), :]
                return total + jnp.dot(
                    left.reshape(4 * CELLS, C), weights[which, t], preferred_element_type=F32
                )

            return step

        def sweep(which, first):
            def body(d, carry):
                start = jnp.zeros((4 * CELLS, 128), F32) if first else acc[d]
                acc[d] = lax.fori_loop(0, TAPS, taps_of(which, d), start, unroll=True)
                return carry

            lax.fori_loop(0, 4, body, 0)

        for zz in range(4):
            p_arrival(0, zz).wait_recv()
            c_copy(1, zz).start()
        sweep(quarter, True)
        for zz in range(4):
            for r in (1, 2):
                p_arrival(r, zz).wait_recv()
                c_copy(1 + r, zz).start()
        for r in (0, 1):
            for zz in range(4):
                c_arrival(r, zz).wait_recv()
        sweep(2 * x + 1 - c, False)
        sweep(across, False)
        for r in (2, 3):
            for zz in range(4):
                c_arrival(r, zz).wait_recv()
        last = 2 * (1 - x) + 1 - c

        def finish(d, carry):
            h, b = d % 2, d // 2
            total = lax.fori_loop(0, TAPS, taps_of(last, d), acc[d], unroll=True)
            stream = kept[pl.ds(h * 8 + b * 4, 4), :, columns(z)].astype(F32)
            total = stream + (total + residual_bias[columns(z)][None, :]).reshape(4, CELLS, 128)
            limit = counts[me % 4 + 4 * h]
            valid = lax.broadcasted_iota(jnp.int32, (4, CELLS, 128), 0) + 4 * b < limit
            done[d] = jnp.where(valid, total, 0.0).astype(BF16).reshape(4 * CELLS, 128)

            @pl.when(d != z)
            def _():
                o_copy(d).start()

            return carry

        lax.fori_loop(0, 4, finish, 0)
        out[:, columns(z)] = done[z]

    for n in range(SLICES):
        @pl.when(n != z)
        def _():
            o_arrival(n).wait_recv()
            z_copy(n).wait_send()

    for to in range(12):
        @pl.when(to != me)
        def _():
            lat_copy(to).wait_send()

    @pl.when(z < SLICES)
    def _():
        for r in range(3):
            for zz in range(4):
                p_copy(r, zz).wait_send()
        for r in range(4):
            for zz in range(4):
                c_copy(r, zz).wait_send()
        for d in range(4):
            @pl.when(d != z)
            def _():
                o_copy(d).wait_send()


def sliced_shards(
    sharded_latents,
    sample_frame_count,
    entry_kernel,
    entry_bias,
    norm_scale_gain,
    residual_kernel,
    residual_bias,
):
    x, me = lax.axis_index("groups"), lax.axis_index("tm")
    c = me % 2
    quarters = jnp.pad(residual_kernel, ((0, 1), (0, 0), (0, 0)))
    mine = lax.dynamic_slice_in_dim(quarters, (2 * x + c) * TAPS, TAPS, 0)
    theirs = lax.dynamic_slice_in_dim(quarters, (2 * x + 1 - c) * TAPS, TAPS, 0)
    received = lax.ppermute(theirs, "tm", [(i, i ^ 1) for i in range(16)])
    low = jnp.where(c == 0, mine, received)
    high = jnp.where(c == 0, received, mine)
    both = jnp.concatenate([low, high], axis=1)
    pieces = jnp.transpose(both.reshape(TAPS, 48, SLICES, 128), (2, 0, 1, 3))

    latq = jnp.transpose(sharded_latents.reshape(4, 4, 4, CELLS), (1, 0, 2, 3)).reshape(4, 16, CELLS)
    latq = jnp.pad(latq, ((0, 0), (0, 0), (0, PLANE - CELLS)))
    vmem = pl.BlockSpec(memory_space=pltpu.VMEM)
    far = pl.BlockSpec(memory_space=pltpu.HBM)
    dma = pltpu.SemaphoreType.DMA
    out = pl.pallas_call(
        section_kernel,
        out_shape=jax.ShapeDtypeStruct((4 * CELLS, C), BF16),
        in_specs=[vmem, pl.BlockSpec(memory_space=pltpu.SMEM)] + [far] * 4 + [vmem],
        out_specs=vmem,
        scratch_shapes=[
            pltpu.VMEM((27 * LATENT_CHANNELS, C), BF16),
            pltpu.VMEM((C,), F32), pltpu.VMEM((C,), F32), pltpu.VMEM((C,), F32),
            pltpu.VMEM((16, 16, PLANE), BF16),
            pltpu.VMEM((2, 10, 144, PLANE), BF16),
            pltpu.VMEM((3, 2, 10, PLANE, C), BF16),
            pltpu.VMEM((16, CELLS, C), BF16),
            pltpu.VMEM((4, TAPS, C, 128), BF16),
            pltpu.VMEM((4, 4 * CELLS, 128), F32),
            pltpu.VMEM((4, 4 * CELLS, 128), BF16),
            dma((12,)), dma((16,)), dma((3,)), dma((4,)), dma((3, 4)), dma((3, 4)),
            dma((4, 4)), dma((4, 4)), dma((4,)), dma((3,)), dma((6,)),
        ],
        compiler_params=pltpu.CompilerParams(
            collective_id=0, has_side_effects=True, vmem_limit_bytes=40 * 1024 * 1024
        ),
        cost_estimate=pl.CostEstimate(flops=5_000_000_000, bytes_accessed=2_000_000, transcendentals=600_000),
    )(
        latq,
        sample_frame_count,
        entry_kernel.reshape(27 * LATENT_CHANNELS, C),
        entry_bias,
        norm_scale_gain,
        residual_bias,
        pieces,
    )
    return out.reshape(4, LATENT_ROWS, LATENT_COLUMNS, C)


def solution(mesh):
    in_specs = (P("groups", "tm"), P("groups"), P(), P(), P(), P(None, "tm", None), P())
    out_specs = P(("groups", "tm"), None, None, None)
    sliced = mesh.shape["groups"] == 2 and mesh.shape["tm"] == 16
    body = sliced_shards if sliced else shards
    return jax.shard_map(body, mesh=mesh, in_specs=in_specs, out_specs=out_specs, check_vma=False)
```

```python
import jax
import jax.numpy as jnp
from jax import lax
from jax.experimental import pallas as pl
from jax.experimental.pallas import tpu as pltpu
from jax.sharding import PartitionSpec as P

LATENT_CHANNELS = 16
C = 384
PROMPT_SAMPLES = 8
BLOCK_FRAMES = 4
LATENT_ROWS = 6
LATENT_COLUMNS = 16


def from_behind(block, axis, distance):
    devices = range(lax.axis_size(axis))
    route = [(i - distance, i) for i in devices if i - distance in devices]
    return lax.ppermute(block, axis, route)


def causal_conv(frames, weight):
    frames_out = frames.shape[0] - 2
    inputs = frames.shape[3]
    padded = jnp.pad(frames, ((0, 0), (1, 1), (1, 1), (0, 0)))
    total = jnp.zeros((frames_out * LATENT_ROWS * LATENT_COLUMNS, weight.shape[2]), jnp.float32)
    for time_tap in range(3):
        for row_tap in range(3):
            for col_tap in range(3):
                window = padded[
                    time_tap : time_tap + frames_out,
                    row_tap : row_tap + LATENT_ROWS,
                    col_tap : col_tap + LATENT_COLUMNS,
                    :,
                ]
                window = window.reshape(frames_out * LATENT_ROWS * LATENT_COLUMNS, inputs)
                tap = 9 * time_tap + 3 * row_tap + col_tap
                total = total + jnp.dot(window, weight[tap], preferred_element_type=jnp.float32)
    return total


def activate(stream, norm_scale_gain):
    values = stream.astype(jnp.float32)
    scale = lax.rsqrt(jnp.mean(values * values, axis=-1, keepdims=True) + 1e-06)
    return jax.nn.silu(values * scale * norm_scale_gain).astype(jnp.bfloat16)


def to_cells(planes):
    return jnp.transpose(
        planes.reshape(planes.shape[0], LATENT_CHANNELS, LATENT_ROWS, LATENT_COLUMNS), (0, 2, 3, 1)
    )


def shards(
    sharded_latents,
    sample_frame_count,
    entry_kernel,
    entry_bias,
    norm_scale_gain,
    residual_kernel,
    residual_bias,
):
    gathered_latents = lax.all_to_all(
        sharded_latents, "tm", split_axis=0, concat_axis=1, tiled=True
    )
    latent_volume = gathered_latents.reshape(
        BLOCK_FRAMES, LATENT_CHANNELS, LATENT_ROWS * LATENT_COLUMNS
    )
    position = lax.axis_index("tm")
    block = position // PROMPT_SAMPLES
    sample = position % PROMPT_SAMPLES
    keep = block > 0
    earlier = from_behind(latent_volume, "tm", PROMPT_SAMPLES)
    earlier = jnp.where(keep, earlier, jnp.zeros_like(earlier))
    frames = to_cells(jnp.concatenate([earlier, latent_volume], axis=0))
    widened = (causal_conv(frames, entry_kernel) + entry_bias).astype(jnp.bfloat16)
    active_all = activate(widened, norm_scale_gain).reshape(
        BLOCK_FRAMES + 2, LATENT_ROWS, LATENT_COLUMNS, C
    )
    behind = jnp.where(keep, active_all[:2], jnp.zeros_like(active_all[:2]))
    extended = jnp.concatenate([behind, active_all[2:]], axis=0)
    stream = widened[2 * LATENT_ROWS * LATENT_COLUMNS :]
    kernel_all = lax.all_gather(residual_kernel, "tm", axis=1, tiled=True)
    branch = causal_conv(extended, kernel_all)
    total = (stream.astype(jnp.float32) + (branch + residual_bias)).reshape(
        BLOCK_FRAMES, LATENT_ROWS, LATENT_COLUMNS, C
    )
    limit = jnp.sum(jnp.where(jnp.arange(PROMPT_SAMPLES) == sample, sample_frame_count, 0))
    frame_index = block * BLOCK_FRAMES + jnp.arange(BLOCK_FRAMES)
    valid = (frame_index < limit)[:, None, None, None]
    return jnp.where(valid, total, jnp.zeros_like(total)).astype(jnp.bfloat16)


MESH = pl.DeviceIdType.MESH
F32, BF16 = jnp.float32, jnp.bfloat16
CELLS = LATENT_ROWS * LATENT_COLUMNS
PLANE = 128
SLICES = 3
TAPS = 7


def section_kernel(
    latq, counts, entry_far, entry_bias_far, gain_far, residual_bias_far, pieces,
    out,
    entry, entry_bias, gain, residual_bias, lat, at, act, kept, weights, acc, done,
    lat_send, lat_recv, z_send, z_recv, p_send, p_recv, c_send, c_recv, o_send, o_recv, own,
):
    x = lax.axis_index("groups")
    me = lax.axis_index("tm")
    z, y, c = me // 4, (me // 2) % 2, me % 2
    quarter = 2 * x + c
    across = 2 * (1 - x) + c

    def where_(zz, yy, cc):
        return {"tm": zz * 4 + yy * 2 + cc}

    peers = [
        {"groups": x, "tm": z * 4 + (1 - y) * 2 + c},
        {"groups": 1 - x, "tm": me},
        {"groups": 1 - x, "tm": z * 4 + (1 - y) * 2 + c},
    ]
    sibling = {"tm": z * 4 + y * 2 + (1 - c)}

    barrier = pltpu.get_barrier_semaphore()
    for step in range(1, 16):
        pl.semaphore_signal(barrier, inc=1, device_id={"tm": lax.rem(me + step, 16)}, device_id_type=MESH)
    for peer in peers[1:]:
        pl.semaphore_signal(barrier, inc=1, device_id=peer, device_id_type=MESH)
    pl.semaphore_wait(barrier, 17)

    def remote(src, dst, send, recv, device):
        return pltpu.make_async_remote_copy(
            src_ref=src, dst_ref=dst, send_sem=send, recv_sem=recv, device_id=device, device_id_type=MESH
        )

    def lat_copy(to):
        return remote(latq.at[to % 4], lat.at[me], lat_send.at[to], lat_recv.at[me], {"tm": to})

    def rows_of(zz, yy):
        return pl.ds(pl.multiple_of(48 * (2 * zz + yy), 16), 48)

    def z_copy(n):
        return remote(
            pieces.at[n], weights.at[quarter, :, rows_of(z, y), :], z_send.at[n], z_recv.at[z], where_(n, y, c)
        )

    def z_arrival(zz):
        return remote(
            pieces.at[0], weights.at[quarter, :, rows_of(zz, y), :], z_send.at[0], z_recv.at[zz], where_(zz, y, c)
        )

    def p_copy(r, zz, source=None):
        block = weights.at[quarter, :, rows_of(zz, y), :]
        return remote(block if source is None else source, block, p_send.at[r, zz], p_recv.at[r, zz], peers[r])

    def p_arrival(r, zz):
        block = weights.at[quarter if r == 0 else across, :, rows_of(zz, y if r == 1 else 1 - y), :]
        return remote(block, block, p_send.at[r, zz], p_recv.at[r, zz], peers[r])

    def c_block(core, r, zz):
        which = 2 * (x if r < 2 else 1 - x) + core
        return weights.at[which, :, rows_of(zz, y if r % 2 == 0 else 1 - y), :]

    def c_copy(r, zz, source=None):
        block = c_block(c, r, zz)
        return remote(block if source is None else source, block, c_send.at[r, zz], c_recv.at[r, zz], sibling)

    def c_arrival(r, zz):
        block = c_block(1 - c, r, zz)
        return remote(block, block, c_send.at[r, zz], c_recv.at[r, zz], sibling)

    def columns(n):
        return pl.ds(pl.multiple_of(128 * n, 128), 128)

    def o_copy(d):
        return remote(done.at[d], out.at[:, columns(z)], o_send.at[d], o_recv.at[z], where_(d, y, c))

    def o_arrival(n):
        return remote(done.at[0], out.at[:, columns(n)], o_send.at[0], o_recv.at[n], where_(n, y, c))

    for to in range(12):
        @pl.when(to != me)
        def _():
            lat_copy(to).start()

    for n in range(SLICES):
        @pl.when(n != z)
        def _():
            z_copy(n).start()

    @pl.when(z < SLICES)
    def _():
        own_piece = pieces.at[lax.rem(z, SLICES)]
        for r in range(3):
            p_copy(r, z, own_piece).start()
        c_copy(0, z, own_piece).start()
        mine = [
            pltpu.make_async_copy(latq.at[me % 4], lat.at[me], own.at[0]),
            pltpu.make_async_copy(own_piece, weights.at[quarter, :, rows_of(z, y), :], own.at[1]),
            pltpu.make_async_copy(entry_far, entry, own.at[2]),
            pltpu.make_async_copy(entry_bias_far, entry_bias, own.at[3]),
            pltpu.make_async_copy(gain_far, gain, own.at[4]),
            pltpu.make_async_copy(residual_bias_far, residual_bias, own.at[5]),
        ]
        for copy in mine:
            copy.start()

        def forward(step):
            near = jnp.where(z == 2, 3 - step, step + jnp.where(step >= z, 1, 0))
            near = jnp.where((z == 2) & (step == 0), 3, near)
            near = jnp.where((z == 2) & (step > 0), 2 - step, near)
            z_arrival(near).wait_recv()
            for r in range(3):
                p_copy(r, near).start()
            c_copy(0, near).start()

        at[:, 0:2] = jnp.zeros((2, 2, 144, PLANE), BF16)
        act[:, :, 0:2] = jnp.zeros((3, 2, 2, PLANE, C), BF16)
        act[:, :, 2:, 0:16] = jnp.zeros((3, 2, 8, 16, C), BF16)
        act[:, :, 2:, 112:128] = jnp.zeros((3, 2, 8, 16, C), BF16)
        forward(0)
        for copy in mine:
            copy.wait()
        for source in range(16):
            @pl.when(source != me)
            def _():
                remote(latq.at[0], lat.at[source], lat_send.at[0], lat_recv.at[source], {"tm": source}).wait_recv()
        target = lax.broadcasted_iota(jnp.int32, (256, 256), 0)
        origin = lax.broadcasted_iota(jnp.int32, (256, 256), 1)
        h_, b_, g_, ch_ = target // 128, (target // 64) % 2, (target // 16) % 4, target % 16
        perm = (origin == (g_ * 4 + ch_ // 4) * 16 + (b_ * 2 + h_) * 4 + ch_ % 4).astype(F32).astype(BF16)
        cells = jnp.dot(perm, lat[...].reshape(256, PLANE), preferred_element_type=F32)
        lane = lax.broadcasted_iota(jnp.int32, (256, PLANE), 1)
        row, column = lane // LATENT_COLUMNS, lane % LATENT_COLUMNS
        for j in range(3):
            for k in range(3):
                offset = (j - 1) * LATENT_COLUMNS + (k - 1)
                moved = pltpu.roll(cells, (-offset) % PLANE, 1) if offset else cells
                good = (
                    (row + (j - 1) >= 0)
                    & (row + (j - 1) < LATENT_ROWS)
                    & (column + (k - 1) >= 0)
                    & (column + (k - 1) < LATENT_COLUMNS)
                )
                tap = 3 * j + k
                at[:, 2:, tap * 16 : tap * 16 + 16, :] = (
                    jnp.where(good, moved, 0.0).astype(BF16).reshape(2, 8, 16, PLANE)
                )

        def inlet(index, carry):
            h, f = index // 8, index % 8
            left = at[h, pl.ds(f, 3)].reshape(432, PLANE)
            wide = lax.dot_general(left, entry[...], (((0,), (0,)), ((), ())), preferred_element_type=F32)
            stream = (wide[:CELLS] + entry_bias[...][None, :]).astype(BF16)
            kept[index] = stream
            values = stream.astype(F32)
            scale = lax.rsqrt(jnp.mean(values * values, axis=-1, keepdims=True) + 1e-06)
            u = values * scale * gain[...][None, :]
            active = (u / (1.0 + jnp.exp(-u))).astype(BF16).astype(F32)
            column = lax.broadcasted_iota(jnp.int32, (CELLS, C), 0) % LATENT_COLUMNS
            act[1, h, 2 + f, 16:112] = active.astype(BF16)
            act[0, h, 2 + f, 16:112] = jnp.where(column == 0, 0.0, pltpu.roll(active, 1, 0)).astype(BF16)
            act[2, h, 2 + f, 16:112] = jnp.where(
                column == LATENT_COLUMNS - 1, 0.0, pltpu.roll(active, CELLS - 1, 0)
            ).astype(BF16)
            return carry

        lax.fori_loop(0, 4, inlet, 0)
        forward(1)
        lax.fori_loop(4, 10, inlet, 0)
        forward(2)
        lax.fori_loop(10, 16, inlet, 0)

        def taps_of(which, d, total):
            h, b = d % 2, d // 2
            for low, count in ((0, 7),):
                lefts = []
                for t in range(low, low + count):
                    tap = jnp.minimum(which * TAPS + t, 26)
                    i, j, k = tap // 9, (tap // 3) % 3, tap % 3
                    left = act[k, h, pl.ds(4 * b + i, 4), pl.ds(pl.multiple_of(16 * j, 16), CELLS), :]
                    lefts.append(left.reshape(4 * CELLS, C))
                right = weights[which, low : low + count].reshape(count * C, 128)
                total = total + jnp.dot(jnp.concatenate(lefts, axis=1), right, preferred_element_type=F32)
            return total

        def sweep(which, first):
            def body(d, carry):
                start = jnp.zeros((4 * CELLS, 128), F32) if first else acc[d]
                acc[d] = taps_of(which, d, start)
                return carry

            lax.fori_loop(0, 4, body, 0)

        for zz in range(4):
            p_arrival(0, zz).wait_recv()
            c_copy(1, zz).start()
        sweep(quarter, True)
        for zz in range(4):
            for r in (1, 2):
                p_arrival(r, zz).wait_recv()
                c_copy(1 + r, zz).start()
        for r in (0, 1):
            for zz in range(4):
                c_arrival(r, zz).wait_recv()
        sweep(2 * x + 1 - c, False)
        sweep(across, False)
        for r in (2, 3):
            for zz in range(4):
                c_arrival(r, zz).wait_recv()
        last = 2 * (1 - x) + 1 - c

        def finish(step, carry):
            middle = jnp.where(step == 0, 3, jnp.where(step == 1, 0, jnp.where(step == 2, 2, 1)))
            upper = jnp.where(step < 2, step, 5 - step)
            d = jnp.where(z == 0, 3 - step, jnp.where(z == 1, middle, upper))
            h, b = d % 2, d // 2
            total = taps_of(last, d, acc[d])
            stream = kept[pl.ds(h * 8 + b * 4, 4), :, columns(z)].astype(F32)
            total = stream + (total + residual_bias[columns(z)][None, :]).reshape(4, CELLS, 128)
            limit = counts[me % 4 + 4 * h]
            valid = lax.broadcasted_iota(jnp.int32, (4, CELLS, 128), 0) + 4 * b < limit
            done[d] = jnp.where(valid, total, 0.0).astype(BF16).reshape(4 * CELLS, 128)

            @pl.when(d != z)
            def _():
                o_copy(d).start()

            return carry

        lax.fori_loop(0, 4, finish, 0)
        out[:, columns(z)] = done[z]

    for n in range(SLICES):
        @pl.when(n != z)
        def _():
            o_arrival(n).wait_recv()
            z_copy(n).wait_send()

    for to in range(12):
        @pl.when(to != me)
        def _():
            lat_copy(to).wait_send()

    @pl.when(z < SLICES)
    def _():
        for r in range(3):
            for zz in range(4):
                p_copy(r, zz).wait_send()
        for r in range(4):
            for zz in range(4):
                c_copy(r, zz).wait_send()
        for d in range(4):
            @pl.when(d != z)
            def _():
                o_copy(d).wait_send()


def sliced_shards(
    sharded_latents,
    sample_frame_count,
    entry_kernel,
    entry_bias,
    norm_scale_gain,
    residual_kernel,
    residual_bias,
):
    x, me = lax.axis_index("groups"), lax.axis_index("tm")
    c = me % 2
    quarters = jnp.pad(residual_kernel, ((0, 1), (0, 0), (0, 0)))
    mine = lax.dynamic_slice_in_dim(quarters, (2 * x + c) * TAPS, TAPS, 0)
    theirs = lax.dynamic_slice_in_dim(quarters, (2 * x + 1 - c) * TAPS, TAPS, 0)
    received = lax.ppermute(theirs, "tm", [(i, i ^ 1) for i in range(16)])
    low = jnp.where(c == 0, mine, received)
    high = jnp.where(c == 0, received, mine)
    both = jnp.concatenate([low, high], axis=1)
    pieces = jnp.transpose(both.reshape(TAPS, 48, SLICES, 128), (2, 0, 1, 3))

    latq = jnp.transpose(sharded_latents.reshape(4, 4, 4, CELLS), (1, 0, 2, 3)).reshape(4, 16, CELLS)
    latq = jnp.pad(latq, ((0, 0), (0, 0), (0, PLANE - CELLS)))
    vmem = pl.BlockSpec(memory_space=pltpu.VMEM)
    far = pl.BlockSpec(memory_space=pltpu.HBM)
    dma = pltpu.SemaphoreType.DMA
    out = pl.pallas_call(
        section_kernel,
        out_shape=jax.ShapeDtypeStruct((4 * CELLS, C), BF16),
        in_specs=[vmem, pl.BlockSpec(memory_space=pltpu.SMEM)] + [far] * 4 + [vmem],
        out_specs=vmem,
        scratch_shapes=[
            pltpu.VMEM((27 * LATENT_CHANNELS, C), BF16),
            pltpu.VMEM((C,), F32), pltpu.VMEM((C,), F32), pltpu.VMEM((C,), F32),
            pltpu.VMEM((16, 16, PLANE), BF16),
            pltpu.VMEM((2, 10, 144, PLANE), BF16),
            pltpu.VMEM((3, 2, 10, PLANE, C), BF16),
            pltpu.VMEM((16, CELLS, C), BF16),
            pltpu.VMEM((4, TAPS, C, 128), BF16),
            pltpu.VMEM((4, 4 * CELLS, 128), F32),
            pltpu.VMEM((4, 4 * CELLS, 128), BF16),
            dma((12,)), dma((16,)), dma((3,)), dma((4,)), dma((3, 4)), dma((3, 4)),
            dma((4, 4)), dma((4, 4)), dma((4,)), dma((3,)), dma((6,)),
        ],
        compiler_params=pltpu.CompilerParams(
            collective_id=0, has_side_effects=True, vmem_limit_bytes=40 * 1024 * 1024
        ),
        cost_estimate=pl.CostEstimate(flops=5_000_000_000, bytes_accessed=2_000_000, transcendentals=600_000),
    )(
        latq,
        sample_frame_count,
        entry_kernel.reshape(27 * LATENT_CHANNELS, C),
        entry_bias,
        norm_scale_gain,
        residual_bias,
        pieces,
    )
    return out.reshape(4, LATENT_ROWS, LATENT_COLUMNS, C)


def solution(mesh):
    in_specs = (P("groups", "tm"), P("groups"), P(), P(), P(), P(None, "tm", None), P())
    out_specs = P(("groups", "tm"), None, None, None)
    sliced = mesh.shape["groups"] == 2 and mesh.shape["tm"] == 16
    body = sliced_shards if sliced else shards
    return jax.shard_map(body, mesh=mesh, in_specs=in_specs, out_specs=out_specs, check_vma=False)
```
